32 devices in a mesh: prow: 4 (over x, core), pcol: 8 (over z, y).
Axes of the slice: x: 2, y: 2, z: 4, core: 2. Of those that a mesh axis runs over, the one named last changes fastest.
Arguments:
- diag_block: float32 [512, 512], P('prow'), as said below
- panel_cols: float32 [8192, 512], P(('prow', 'pcol')), may hold values from -3 to 3
- trailing: float32 [8192, 8192], P('prow', 'pcol'), may hold values from -6 to 6
- geno_top: float32 [512, 2048], P('prow', 'pcol'), may hold values from -6 to 6
- geno_rest: float32 [8192, 2048], P('prow', 'pcol'), may hold values from -6 to 6
- pheno_top: float32 [512], P('prow'), may hold values from -6 to 6
- pheno_rest: float32 [8192], P('prow'), may hold values from -6 to 6
Outputs:
- updated_block: float32 [8192, 8192], P('prow', 'pcol')
- panel_factor: float32 [8192, 512], P(('prow', 'pcol'))
- white_geno: float32 [8192, 2048], P('prow', 'pcol')
- score_stat: float32 [2048], P('pcol')
- info_stat: float32 [2048], P('pcol')
The draws below stay inside these ranges and needn't reach their ends.
Inputs may be any that keep to these rules, and one draw needn't show every extreme that they name: diag_block is symmetric and positive definite; its diagonal entries lie between 3 and 4.5 and its off-diagonal entries have magnitude at most 0.8.
All inputs are finite; a program needn't handle non-finite values.
Results may differ from the reference program's by a relative error of at most 0.000096.
Values sent between devices are 32-bit elements; how exact they have to be, the bound alone decides.
A program may use at most 64 MiB of HBM per device.

```python
import jax
import jax.numpy as jnp
from jax import lax

NB = 512
ROWS = 8192
VARIANTS = 2048


def draw_diag_block(key, part):
    key_scale, key_noise, key_diag = jax.random.split(key, 3)
    row_scales = jax.random.uniform(key_scale, (NB,), jnp.float32, 0.6, 1.25)
    noise_vals = jax.random.uniform(key_noise, (NB, NB), jnp.float32, -1.0, 1.0)
    positions = jnp.arange(NB).astype(jnp.float32)
    reach = jnp.float32(NB) / 16.0
    kernel = jnp.exp(-jnp.abs(positions[:, None] - positions[None, :]) / reach)
    coupled = 0.5 * row_scales[:, None] * row_scales[None, :] * kernel
    rough = 0.15 * (noise_vals + noise_vals.T) / jnp.float32(NB)
    diag_vals = jax.random.uniform(key_diag, (NB,), jnp.float32, 3.0, 4.5)
    identity = jnp.eye(NB, dtype=jnp.float32)
    return (coupled + rough) * (1.0 - identity) + identity * diag_vals[:, None]


def steps_of(key, dims, shards, low, top_value):
    def one(dim, parts):
        heights = jax.random.uniform(jax.random.fold_in(jax.random.fold_in(key, 6), dim), (parts,), jnp.float32, low / len(shards), top_value / len(shards))
        return jnp.repeat(jnp.exp(heights), dims[dim] // parts).reshape((-1,) + (1,) * (len(dims) - dim - 1))

    level = one(*shards[0])
    for cut in shards[1:]:
        level = level * one(*cut)
    return level


def centred(rng, extent, scale, bound, cuts=(), held_as=jnp.bfloat16):
    array = jax.random.normal(rng, extent, jnp.float32) * scale
    if len(cuts) > 0:
        array = steps_of(rng, extent, cuts, -0.22, 0.18) * array
    return jnp.clip(array, min=-bound, max=bound).astype(held_as)


def setup_inputs(seed: int = 0) -> dict:
    key_of = jax.random.split(jax.random.key(seed), 8)
    return {
        "diag_block": draw_diag_block(jax.random.fold_in(key_of[7], 71), 0),
        "panel_cols": centred(key_of[1], (ROWS, NB), 0.2, 3.0, ((0, 32),), jnp.float32),
        "trailing": centred(key_of[2], (ROWS, ROWS), 1.0, 6.0, ((0, 4), (1, 8)), jnp.float32),
        "geno_top": centred(key_of[3], (NB, VARIANTS), 1.0, 6.0, ((0, 4), (1, 8)), jnp.float32),
        "geno_rest": centred(key_of[4], (ROWS, VARIANTS), 1.0, 6.0, ((0, 4), (1, 8)), jnp.float32),
        "pheno_top": centred(key_of[5], (NB,), 1.0, 6.0, ((0, 4),), jnp.float32),
        "pheno_rest": centred(key_of[6], (ROWS,), 1.0, 6.0, ((0, 4),), jnp.float32),
    }


def reference(diag_block, panel_cols, trailing, geno_top, geno_rest, pheno_top, pheno_rest):
    highest = lax.Precision.HIGHEST
    factor = jnp.linalg.cholesky(diag_block)
    panel_factor = lax.linalg.triangular_solve(factor, panel_cols, left_side=False, lower=True, transpose_a=True)
    updated_block = trailing - jnp.dot(panel_factor, panel_factor.T, precision=highest)
    top_white = lax.linalg.triangular_solve(factor, geno_top, left_side=True, lower=True)
    pheno_white_top = lax.linalg.triangular_solve(factor, pheno_top[:, None], left_side=True, lower=True)[:, 0]
    white_geno = geno_rest - jnp.dot(panel_factor, top_white, precision=highest)
    pheno_white = pheno_rest - jnp.dot(panel_factor, pheno_white_top, precision=highest)
    count = NB + ROWS
    score_stat = (jnp.dot(pheno_white, white_geno, precision=highest) + jnp.dot(pheno_white_top, top_white, precision=highest)) / jnp.sqrt(jnp.float32(count))
    info_stat = (lax.optimization_barrier(jnp.sum(white_geno * white_geno, axis=0)) + lax.optimization_barrier(jnp.sum(top_white * top_white, axis=0))) / jnp.float32(count)
    return (updated_block, panel_factor, white_geno, score_stat, info_stat)
```

```python
import functools

import jax
import jax.numpy as jnp
from jax import lax
from jax.experimental import pallas as pl
from jax.experimental.pallas import tpu as pltpu
from jax.sharding import PartitionSpec as P

MESH = pl.DeviceIdType.MESH
HIGHEST = lax.Precision.HIGHEST
TILE = 8
BLOCK = 128


def split3(value):
    hi = value.astype(jnp.bfloat16).astype(jnp.float32)
    rest = value - hi
    mid = rest.astype(jnp.bfloat16).astype(jnp.float32)
    return hi, mid, rest - mid


def tile_step(m_ref, step):
    start = pl.multiple_of(step * TILE, TILE)
    left = m_ref[pl.ds(start, TILE), :BLOCK]
    right = m_ref[pl.ds(start, TILE), BLOCK:]
    rolled = pltpu.roll(left, lax.rem(BLOCK - start, BLOCK), 1)
    cols = [jnp.broadcast_to(rolled[:, k : k + 1], (TILE, BLOCK)) for k in range(TILE)]
    rows = lax.broadcasted_iota(jnp.int32, (TILE, BLOCK), 0)
    lanes = lax.broadcasted_iota(jnp.int32, (TILE, BLOCK), 1)
    for j in range(TILE):
        inv = lax.rsqrt(jnp.broadcast_to(cols[j][j : j + 1, :], (TILE, BLOCK)))
        factor = jnp.where(rows > j, cols[j] * inv, 0.0)

        def work(value):
            scaled = jnp.broadcast_to(value[j : j + 1, :], (TILE, BLOCK)) * inv
            return jnp.where(rows == j, scaled, value - factor * scaled)

        left, right = work(left), work(right)
        for k in range(j + 1, TILE):
            cols[k] = work(cols[k])
    m_ref[pl.ds(start, TILE), :BLOCK] = left
    m_ref[pl.ds(start, TILE), BLOCK:] = right
    both = jnp.concatenate([left, right], axis=1)
    mult = jnp.where(lanes >= start + TILE, left, 0.0)
    a0, a1, a2 = split3(mult)
    b0, b1, b2 = split3(both)
    lhs = jnp.concatenate([a0, a0, a1, a0, a1, a2], axis=0).astype(jnp.bfloat16)
    rhs = jnp.concatenate([b0, b1, b0, b2, b1, b0], axis=0).astype(jnp.bfloat16)
    m_ref[...] -= lax.dot_general(
        lhs, rhs, (((0,), (0,)), ((), ())), preferred_element_type=jnp.float32
    )


def dot_t(a, b):
    return lax.dot_general(
        a, b, (((0,), (0,)), ((), ())), precision=HIGHEST, preferred_element_type=jnp.float32
    )


def dot_n(a, b):
    return jnp.dot(a, b, precision=HIGHEST, preferred_element_type=jnp.float32)


def invert(a_ref, w_ref, m_ref, events):
    width = a_ref.shape[0]
    blocks = width // BLOCK
    tiles = BLOCK // TILE
    w_ref[...] = jnp.zeros_like(w_ref)
    eye = (
        lax.broadcasted_iota(jnp.int32, (BLOCK, BLOCK), 0)
        == lax.broadcasted_iota(jnp.int32, (BLOCK, BLOCK), 1)
    ).astype(jnp.float32)
    slot = 0
    for k in range(blocks):
        lo, hi = k * BLOCK, (k + 1) * BLOCK
        m_ref[:, :BLOCK] = a_ref[lo:hi, lo:hi]
        m_ref[:, BLOCK:] = eye
        for part in range(2):

            def body(step, carry):
                tile_step(m_ref, step)
                return carry

            lax.fori_loop(part * tiles // 2, (part + 1) * tiles // 2, body, 0)
            if part == 0:
                if slot < len(events):
                    events[slot]()
                slot += 1
        own = m_ref[:, BLOCK:]
        if k > 0:
            w_ref[lo:hi, :lo] = dot_n(own, w_ref[lo:hi, :lo])
        w_ref[lo:hi, lo:hi] = own
        if k < blocks - 1:
            upper = dot_n(own, a_ref[lo:hi, hi:])
            a_ref[hi:, hi:] -= dot_t(upper, upper)
            w_ref[hi:, :hi] -= dot_t(upper, w_ref[lo:hi, :hi])
        if slot < len(events):
            events[slot]()
        slot += 1
    while slot < len(events):
        events[slot]()
        slot += 1


def gather_kernel(
    ly, lz, group,
    diag_in, top_in, panel_in,
    w_out, row_out, col_out, top_out,
    a_ref, m_ref,
    barrier_free, small_send, small_recv, row_send, row_recv, col_send, col_recv, local_sem,
):
    r, c = lax.axis_index("prow"), lax.axis_index("pcol")
    z, y = c // ly, lax.rem(c, ly)
    sib = r + 1 - 2 * lax.rem(r, 2)
    cross = r + 2 - 4 * (r // 2)
    diag_x = sib + 2 - 4 * (sib // 2)
    other = z * ly + (1 - y)
    col_parts = col_out.shape[0]
    root = c // group
    first = lax.rem(c, group) * col_parts
    is_root = root == r
    root_sib = root + 1 - 2 * lax.rem(root, 2)
    root_cross = root + 2 - 4 * (root // 2)
    del barrier_free

    barrier = pltpu.get_barrier_semaphore()

    def greet(row, col):
        pl.semaphore_signal(barrier, inc=1, device_id={"prow": row, "pcol": col}, device_id_type=MESH)

    greet(sib, c)
    greet(cross, c)
    greet(r, other)

    @pl.when(z > 0)
    def _():
        greet(r, c - ly)

    @pl.when(z < lz - 1)
    def _():
        greet(r, c + ly)

    pl.semaphore_wait(barrier, 3 + jnp.minimum(z, 1) + jnp.minimum(lz - 1 - z, 1))

    def remote(src, dst, send, recv, row, col):
        return pltpu.make_async_remote_copy(
            src_ref=src, dst_ref=dst, send_sem=send, recv_sem=recv,
            device_id={"prow": row, "pcol": col}, device_id_type=MESH,
        )

    height = diag_in.shape[0]

    def diag_at(q):
        return a_ref.at[pl.ds(pl.multiple_of(q * height, height), height), :]

    def small(kind, lane):
        source = diag_in if kind == 0 else top_in
        place = diag_at if kind == 0 else (lambda q: top_out.at[q])
        part = cross if lane == 2 else r
        src = place(part) if lane == 2 else source
        return remote(
            src, place(part), small_send.at[kind, lane], small_recv.at[kind, part],
            cross if lane == 1 else sib, c,
        )

    def small_wait(kind, part):
        place = diag_at if kind == 0 else (lambda q: top_out.at[q])
        remote(place(part), place(part), small_send.at[kind, 0], small_recv.at[kind, part], sib, c).wait_recv()

    def row_copy(way, b, own):
        target = (c + ly, c - ly, other)[way]
        return remote(
            panel_in if own else row_out.at[b], row_out.at[b],
            row_send.at[way, b], row_recv.at[b], r, target,
        )

    def row_wait(b):
        remote(row_out.at[b], row_out.at[b], row_send.at[0, b], row_recv.at[b], r, other).wait_recv()

    def col_copies(b, own):
        i = b - first
        src = panel_in if own else row_out.at[b]
        return (
            remote(src, col_out.at[i], col_send.at[0, i], col_recv.at[i], cross, c),
            remote(src, col_out.at[i], col_send.at[1, i], col_recv.at[i], sib, c),
            pltpu.make_async_copy(src, col_out.at[i], local_sem.at[1 + i]),
        )

    def in_col(b):
        return is_root & (b >= first) & (b < first + col_parts)

    def col_start(b, own):
        @pl.when(in_col(b))
        def _():
            for copy in col_copies(b, own):
                copy.start()

    def col_finish(b, own):
        @pl.when(in_col(b))
        def _():
            one, two, three = col_copies(b, own)
            one.wait_send()
            two.wait_send()
            three.wait()

    def up(fn):
        pl.when(z < lz - 1)(fn)

    def down(fn):
        pl.when(z > 0)(fn)

    small(0, 1).start()
    small(0, 0).start()
    row_copy(2, c, True).start()
    up(lambda: row_copy(0, c, True).start())
    down(lambda: row_copy(1, c, True).start())
    small(1, 1).start()
    small(1, 0).start()
    own_copy = pltpu.make_async_copy(panel_in, row_out.at[c], local_sem.at[0])
    own_copy.start()
    top_copy = pltpu.make_async_copy(top_in, top_out.at[r], local_sem.at[1 + col_parts])
    top_copy.start()
    col_start(c, True)
    a_ref[pl.ds(pl.multiple_of(r * height, height), height), :] = diag_in[...]
    small_wait(0, cross)
    small(0, 2).start()
    small_wait(0, sib)
    small_wait(0, diag_x)
    small(0, 2).wait_send()

    def hop(d):
        low, high = c - d * ly, c + d * ly

        @pl.when(z >= d)
        def _():
            row_wait(low)
            up(lambda: row_copy(0, low, False).start())
            row_copy(2, low, False).start()
            col_start(low, False)

        @pl.when(z + d < lz)
        def _():
            row_wait(high)
            down(lambda: row_copy(1, high, False).start())
            row_copy(2, high, False).start()
            col_start(high, False)

    def across(d):
        def one(b):
            row_wait(b)
            col_start(b, False)

        if d == 0:
            one(other)
        else:
            pl.when(z >= d)(lambda: one(other - d * ly))
            pl.when(z + d < lz)(lambda: one(other + d * ly))

    def top_event():
        small_wait(1, cross)
        small(1, 2).start()

    def first_event():
        hop(1)
        across(0)

    def make(d):
        def run():
            if d < lz:
                hop(d)
            across(d - 1)

        return run

    def nothing():
        pass

    events = [first_event, top_event, make(2), nothing, make(3), nothing, nothing]
    events += [make(d) for d in range(4, lz + 1)]
    invert(a_ref, w_out, m_ref, events)

    def handed(i):
        return remote(col_out.at[i], col_out.at[i], col_send.at[1, i], col_recv.at[i], sib, c)

    @pl.when(r == root_cross)
    def _():
        for i in range(col_parts):
            handed(i).wait_recv()
            handed(i).start()
        for i in range(col_parts):
            handed(i).wait_send()

    @pl.when(jnp.logical_not(is_root) & (r != root_cross))
    def _():
        for i in range(col_parts):
            handed(i).wait_recv()

    del root_sib
    small(0, 1).wait_send()
    small(0, 0).wait_send()
    small(1, 1).wait_send()
    small(1, 0).wait_send()
    small(1, 2).wait_send()
    small_wait(1, sib)
    small_wait(1, diag_x)
    own_copy.wait()
    top_copy.wait()
    row_copy(2, c, True).wait_send()
    up(lambda: row_copy(0, c, True).wait_send())
    down(lambda: row_copy(1, c, True).wait_send())
    col_finish(c, True)
    col_finish(other, False)
    for d in range(1, lz):

        @pl.when(z >= d)
        def _():
            low = c - d * ly
            up(lambda: row_copy(0, low, False).wait_send())
            row_copy(2, low, False).wait_send()
            col_finish(low, False)
            col_finish(other - d * ly, False)

        @pl.when(z + d < lz)
        def _():
            high = c + d * ly
            down(lambda: row_copy(1, high, False).wait_send())
            row_copy(2, high, False).wait_send()
            col_finish(high, False)
            col_finish(other + d * ly, False)


def gather_and_invert(diag_block, top_aug, panel_cols, prow_size, pcol_size):
    ly = 2
    lz = pcol_size // ly
    height, width = diag_block.shape
    rows_piece = panel_cols.shape[0]
    col_parts = prow_size
    any_spec = pl.BlockSpec(memory_space=pl.ANY)
    vmem = pl.BlockSpec(memory_space=pltpu.VMEM)
    dma = pltpu.SemaphoreType.DMA
    f32 = jnp.float32
    return pl.pallas_call(
        functools.partial(gather_kernel, ly, lz, pcol_size // prow_size),
        out_shape=(
            jax.ShapeDtypeStruct((width, width), f32),
            jax.ShapeDtypeStruct((pcol_size, rows_piece, width), f32),
            jax.ShapeDtypeStruct((col_parts, rows_piece, width), f32),
            jax.ShapeDtypeStruct((prow_size,) + top_aug.shape, f32),
        ),
        in_specs=[vmem, any_spec, any_spec],
        out_specs=(vmem, any_spec, any_spec, any_spec),
        scratch_shapes=[
            pltpu.VMEM((width, width), f32),
            pltpu.VMEM((BLOCK, 2 * BLOCK), f32),
            pltpu.SemaphoreType.REGULAR,
            dma((2, 3)),
            dma((2, prow_size)),
            dma((3, pcol_size)),
            dma((pcol_size,)),
            dma((2, col_parts)),
            dma((col_parts,)),
            dma((2 + col_parts,)),
        ],
        compiler_params=pltpu.CompilerParams(
            collective_id=0, has_side_effects=True, vmem_limit_bytes=24 * 1024 * 1024
        ),
    )(diag_block, top_aug, panel_cols)


def dot3(a, b, dims):
    return lax.dot_general(a, b, (dims, ((), ())), precision=lax.Precision.HIGH)


def local(diag_block, panel_cols, trailing, geno_top, geno_rest, pheno_top, pheno_rest):
    prow_size, pcol_size = lax.axis_size("prow"), lax.axis_size("pcol")
    height, width = diag_block.shape
    rows_piece = panel_cols.shape[0]
    row_count = rows_piece * pcol_size
    variants = geno_top.shape[1]
    pad = jnp.broadcast_to(pheno_top[:, None], (height, BLOCK))
    top_aug = jnp.concatenate([geno_top, pad], axis=1)
    inverse, whole, col_raw, top_all = gather_and_invert(
        diag_block, top_aug, panel_cols, prow_size, pcol_size
    )
    whole = whole.reshape(row_count, width)
    col_raw = col_raw.reshape(-1, width)
    top_all = top_all.reshape(width, variants + BLOCK)
    white_aug = dot3(inverse, top_all, ((1,), (0,)))
    panel_rows = dot3(whole, inverse, ((1,), (1,)))
    col_panel = dot3(col_raw, inverse, ((1,), (1,)))
    own_factor = lax.dynamic_slice_in_dim(
        panel_rows, lax.axis_index("pcol") * rows_piece, rows_piece, 0
    )
    top_white, pheno_white_top = white_aug[:, :variants], white_aug[:, variants]
    shift = dot3(panel_rows, white_aug, ((1,), (0,)))
    white_geno = geno_rest - shift[:, :variants]
    pheno_white = pheno_rest - shift[:, variants]
    part_score = jnp.dot(pheno_white, white_geno, precision=HIGHEST)
    part_info = jnp.sum(white_geno * white_geno, axis=0)
    score_sum, info_sum = lax.psum((part_score, part_info), "prow")
    updated_block = trailing - dot3(panel_rows, col_panel, ((1,), (1,)))
    count = width + row_count * prow_size
    score_stat = (score_sum + jnp.dot(pheno_white_top, top_white, precision=HIGHEST)) / jnp.sqrt(
        jnp.float32(count)
    )
    info_stat = (info_sum + jnp.sum(top_white * top_white, axis=0)) / jnp.float32(count)
    return (updated_block, own_factor, white_geno, score_stat, info_stat)


def solution(mesh):
    placed = (
        P("prow", None),
        P(("prow", "pcol"), None),
        P("prow", "pcol"),
        P("prow", "pcol"),
        P("prow", "pcol"),
        P("prow"),
        P("prow"),
    )
    return jax.shard_map(
        local,
        mesh=mesh,
        in_specs=placed,
        out_specs=(
            P("prow", "pcol"),
            P(("prow", "pcol"), None),
            P("prow", "pcol"),
            P("pcol"),
            P("pcol"),
        ),
        check_vma=False,
    )
```

```python
import functools

import jax
import jax.numpy as jnp
from jax import lax
from jax.experimental import pallas as pl
from jax.experimental.pallas import tpu as pltpu
from jax.sharding import PartitionSpec as P

MESH = pl.DeviceIdType.MESH
HIGHEST = lax.Precision.HIGHEST
TILE = 8
BLOCK = 128


def split3(value):
    hi = value.astype(jnp.bfloat16).astype(jnp.float32)
    rest = value - hi
    mid = rest.astype(jnp.bfloat16).astype(jnp.float32)
    return hi, mid, rest - mid


def tile_step(m_ref, step):
    start = pl.multiple_of(step * TILE, TILE)
    left = m_ref[pl.ds(start, TILE), :BLOCK]
    right = m_ref[pl.ds(start, TILE), BLOCK:]
    rolled = pltpu.roll(left, lax.rem(BLOCK - start, BLOCK), 1)
    cols = [jnp.broadcast_to(rolled[:, k : k + 1], (TILE, BLOCK)) for k in range(TILE)]
    rows = lax.broadcasted_iota(jnp.int32, (TILE, BLOCK), 0)
    lanes = lax.broadcasted_iota(jnp.int32, (TILE, BLOCK), 1)
    for j in range(TILE):
        pivot = jnp.broadcast_to(cols[j][j : j + 1, :], (TILE, BLOCK))
        inv = lax.rsqrt(pivot)
        inv = inv * (1.5 - (0.5 * pivot) * inv * inv)
        factor = jnp.where(rows > j, cols[j] * inv, 0.0)

        def work(value):
            scaled = jnp.broadcast_to(value[j : j + 1, :], (TILE, BLOCK)) * inv
            return jnp.where(rows == j, scaled, value - factor * scaled)

        left, right = work(left), work(right)
        for k in range(j + 1, TILE):
            cols[k] = work(cols[k])
    m_ref[pl.ds(start, TILE), :BLOCK] = left
    m_ref[pl.ds(start, TILE), BLOCK:] = right
    both = jnp.concatenate([left, right], axis=1)
    mult = jnp.where(lanes >= start + TILE, left, 0.0)
    a0, a1, a2 = split3(mult)
    b0, b1, b2 = split3(both)
    lhs = jnp.concatenate([a0, a0, a1, a0, a1, a2], axis=0).astype(jnp.bfloat16)
    rhs = jnp.concatenate([b0, b1, b0, b2, b1, b0], axis=0).astype(jnp.bfloat16)
    m_ref[...] -= lax.dot_general(
        lhs, rhs, (((0,), (0,)), ((), ())), preferred_element_type=jnp.float32
    )


def dot_t(a, b):
    return lax.dot_general(
        a, b, (((0,), (0,)), ((), ())), precision=HIGHEST, preferred_element_type=jnp.float32
    )


def dot_n(a, b):
    return jnp.dot(a, b, precision=HIGHEST, preferred_element_type=jnp.float32)


def invert(a_ref, w_ref, m_ref, events):
    width = a_ref.shape[0]
    blocks = width // BLOCK
    tiles = BLOCK // TILE
    w_ref[...] = jnp.zeros_like(w_ref)
    eye = (
        lax.broadcasted_iota(jnp.int32, (BLOCK, BLOCK), 0)
        == lax.broadcasted_iota(jnp.int32, (BLOCK, BLOCK), 1)
    ).astype(jnp.float32)
    slot = 0
    for k in range(blocks):
        lo, hi = k * BLOCK, (k + 1) * BLOCK
        m_ref[:, :BLOCK] = a_ref[lo:hi, lo:hi]
        m_ref[:, BLOCK:] = eye
        for part in range(2):

            def body(step, carry):
                tile_step(m_ref, step)
                return carry

            lax.fori_loop(part * tiles // 2, (part + 1) * tiles // 2, body, 0)
            if part == 0:
                if slot < len(events):
                    events[slot]()
                slot += 1
        own = m_ref[:, BLOCK:]
        if k > 0:
            w_ref[lo:hi, :lo] = dot_n(own, w_ref[lo:hi, :lo])
        w_ref[lo:hi, lo:hi] = own
        if k < blocks - 1:
            upper = dot_n(own, a_ref[lo:hi, hi:])
            a_ref[hi:, hi:] -= dot_t(upper, upper)
            w_ref[hi:, :hi] -= dot_t(upper, w_ref[lo:hi, :hi])
        if slot < len(events):
            events[slot]()
        slot += 1
    while slot < len(events):
        events[slot]()
        slot += 1


def gather_kernel(
    ly, lz, group,
    diag_in, top_in, pheno_in, panel_in,
    w_out, row_out, col_out, top_out, pheno_out,
    a_ref, m_ref,
    small_send, small_recv, row_send, row_recv, col_send, col_recv, local_sem,
):
    r, c = lax.axis_index("prow"), lax.axis_index("pcol")
    z, y = c // ly, lax.rem(c, ly)
    sib = r + 1 - 2 * lax.rem(r, 2)
    cross = r + 2 - 4 * (r // 2)
    diag_x = sib + 2 - 4 * (sib // 2)
    other = z * ly + (1 - y)
    col_parts = col_out.shape[0]
    root = c // group
    first = lax.rem(c, group) * col_parts
    is_root = root == r
    root_cross = root + 2 - 4 * (root // 2)

    barrier = pltpu.get_barrier_semaphore()

    def greet(row, col):
        pl.semaphore_signal(barrier, inc=1, device_id={"prow": row, "pcol": col}, device_id_type=MESH)

    greet(sib, c)
    greet(cross, c)
    greet(r, other)

    @pl.when(z > 0)
    def _():
        greet(r, c - ly)

    @pl.when(z < lz - 1)
    def _():
        greet(r, c + ly)

    pl.semaphore_wait(barrier, 3 + jnp.minimum(z, 1) + jnp.minimum(lz - 1 - z, 1))

    def remote(src, dst, send, recv, row, col):
        return pltpu.make_async_remote_copy(
            src_ref=src, dst_ref=dst, send_sem=send, recv_sem=recv,
            device_id={"prow": row, "pcol": col}, device_id_type=MESH,
        )

    height = diag_in.shape[0]

    def diag_at(q):
        return a_ref.at[pl.ds(pl.multiple_of(q * height, height), height), :]

    places = (diag_at, lambda q: top_out.at[q], lambda q: pheno_out.at[q])

    def small(kind, lane):
        source = (diag_in, top_in, pheno_in)[kind]
        place = places[kind]
        part = cross if lane == 2 else r
        src = place(part) if lane == 2 else source
        return remote(
            src, place(part), small_send.at[kind, lane], small_recv.at[kind, part],
            cross if lane == 1 else sib, c,
        )

    def small_wait(kind, part):
        place = places[kind]
        remote(place(part), place(part), small_send.at[kind, 0], small_recv.at[kind, part], sib, c).wait_recv()

    def row_copy(way, b, own):
        target = (c + ly, c - ly, other)[way]
        return remote(
            panel_in if own else row_out.at[b], row_out.at[b],
            row_send.at[way, b], row_recv.at[b], r, target,
        )

    def row_wait(b):
        remote(row_out.at[b], row_out.at[b], row_send.at[0, b], row_recv.at[b], r, other).wait_recv()

    def col_copies(b, own):
        i = b - first
        src = panel_in if own else row_out.at[b]
        return (
            remote(src, col_out.at[i], col_send.at[0, i], col_recv.at[i], cross, c),
            remote(src, col_out.at[i], col_send.at[1, i], col_recv.at[i], sib, c),
            pltpu.make_async_copy(src, col_out.at[i], local_sem.at[1 + i]),
        )

    def in_col(b):
        return is_root & (b >= first) & (b < first + col_parts)

    def col_start(b, own):
        @pl.when(in_col(b))
        def _():
            for copy in col_copies(b, own):
                copy.start()

    def col_finish(b, own):
        @pl.when(in_col(b))
        def _():
            one, two, three = col_copies(b, own)
            one.wait_send()
            two.wait_send()
            three.wait()

    def up(fn):
        pl.when(z < lz - 1)(fn)

    def down(fn):
        pl.when(z > 0)(fn)

    small(0, 1).start()
    small(0, 0).start()
    row_copy(2, c, True).start()
    up(lambda: row_copy(0, c, True).start())
    down(lambda: row_copy(1, c, True).start())
    for kind in (1, 2):
        small(kind, 1).start()
        small(kind, 0).start()
    own_copy = pltpu.make_async_copy(panel_in, row_out.at[c], local_sem.at[0])
    own_copy.start()
    top_copy = pltpu.make_async_copy(top_in, top_out.at[r], local_sem.at[1 + col_parts])
    top_copy.start()
    pheno_copy = pltpu.make_async_copy(pheno_in, pheno_out.at[r], local_sem.at[2 + col_parts])
    pheno_copy.start()
    diag_copy = pltpu.make_async_copy(diag_in, diag_at(r), local_sem.at[3 + col_parts])
    diag_copy.start()
    col_start(c, True)
    small_wait(0, cross)
    small(0, 2).start()
    small_wait(0, sib)
    small_wait(0, diag_x)
    diag_copy.wait()
    small(0, 2).wait_send()

    def hop(d):
        low, high = c - d * ly, c + d * ly

        @pl.when(z >= d)
        def _():
            row_wait(low)
            up(lambda: row_copy(0, low, False).start())
            row_copy(2, low, False).start()
            col_start(low, False)

        @pl.when(z + d < lz)
        def _():
            row_wait(high)
            down(lambda: row_copy(1, high, False).start())
            row_copy(2, high, False).start()
            col_start(high, False)

    def across(d):
        def one(b):
            row_wait(b)
            col_start(b, False)

        if d == 0:
            one(other)
        else:
            pl.when(z >= d)(lambda: one(other - d * ly))
            pl.when(z + d < lz)(lambda: one(other + d * ly))

    def top_event():
        for kind in (1, 2):
            small_wait(kind, cross)
            small(kind, 2).start()

    def first_event():
        hop(1)
        across(0)

    def make(d):
        def run():
            if d < lz:
                hop(d)
            across(d - 1)

        return run

    def nothing():
        pass

    events = [first_event, top_event, make(2), nothing, make(3), nothing, nothing]
    events += [make(d) for d in range(4, lz + 1)]
    invert(a_ref, w_out, m_ref, events)

    def handed(i):
        return remote(col_out.at[i], col_out.at[i], col_send.at[1, i], col_recv.at[i], sib, c)

    @pl.when(r == root_cross)
    def _():
        for i in range(col_parts):
            handed(i).wait_recv()
            handed(i).start()
        for i in range(col_parts):
            handed(i).wait_send()

    @pl.when(jnp.logical_not(is_root) & (r != root_cross))
    def _():
        for i in range(col_parts):
            handed(i).wait_recv()

    small(0, 1).wait_send()
    small(0, 0).wait_send()
    for kind in (1, 2):
        for lane in range(3):
            small(kind, lane).wait_send()
        small_wait(kind, sib)
        small_wait(kind, diag_x)
    own_copy.wait()
    top_copy.wait()
    pheno_copy.wait()
    row_copy(2, c, True).wait_send()
    up(lambda: row_copy(0, c, True).wait_send())
    down(lambda: row_copy(1, c, True).wait_send())
    col_finish(c, True)
    col_finish(other, False)
    for d in range(1, lz):

        @pl.when(z >= d)
        def _():
            low = c - d * ly
            up(lambda: row_copy(0, low, False).wait_send())
            row_copy(2, low, False).wait_send()
            col_finish(low, False)
            col_finish(other - d * ly, False)

        @pl.when(z + d < lz)
        def _():
            high = c + d * ly
            down(lambda: row_copy(1, high, False).wait_send())
            row_copy(2, high, False).wait_send()
            col_finish(high, False)
            col_finish(other + d * ly, False)


def gather_and_invert(diag_block, geno_top, pheno_row, panel_cols, prow_size, pcol_size):
    ly = 2
    lz = pcol_size // ly
    height, width = diag_block.shape
    rows_piece = panel_cols.shape[0]
    col_parts = prow_size
    any_spec = pl.BlockSpec(memory_space=pl.ANY)
    vmem = pl.BlockSpec(memory_space=pltpu.VMEM)
    dma = pltpu.SemaphoreType.DMA
    f32 = jnp.float32
    return pl.pallas_call(
        functools.partial(gather_kernel, ly, lz, pcol_size // prow_size),
        out_shape=(
            jax.ShapeDtypeStruct((width, width), f32),
            jax.ShapeDtypeStruct((pcol_size, rows_piece, width), f32),
            jax.ShapeDtypeStruct((col_parts, rows_piece, width), f32),
            jax.ShapeDtypeStruct((prow_size,) + geno_top.shape, f32),
            jax.ShapeDtypeStruct((prow_size,) + pheno_row.shape, f32),
        ),
        in_specs=[any_spec] * 4,
        out_specs=(vmem, any_spec, any_spec, any_spec, any_spec),
        scratch_shapes=[
            pltpu.VMEM((width, width), f32),
            pltpu.VMEM((BLOCK, 2 * BLOCK), f32),
            dma((3, 3)),
            dma((3, prow_size)),
            dma((3, pcol_size)),
            dma((pcol_size,)),
            dma((2, col_parts)),
            dma((col_parts,)),
            dma((4 + col_parts,)),
        ],
        compiler_params=pltpu.CompilerParams(
            collective_id=0, has_side_effects=True, vmem_limit_bytes=56 * 1024 * 1024
        ),
    )(diag_block, geno_top, pheno_row, panel_cols)


LAST = ((1,), (1,))
INNER = ((1,), (0,))


def split2(value):
    hi = value.astype(jnp.bfloat16)
    return hi, (value - hi.astype(jnp.float32)).astype(jnp.bfloat16)


def dot3(a, b, dims):
    def one(x, y):
        return lax.dot_general(x, y, (dims, ((), ())), preferred_element_type=jnp.float32)

    return one(a[0], b[0]) + (one(a[0], b[1]) + one(a[1], b[0]))


def whiten_kernel(
    tile, pieces, col_tiles,
    w_in, top_in, pheno_in, rows_in, cols_in, geno_in, rest_in,
    hi_out, lo_out, col_hi_out, col_lo_out, own_out, geno_out, stat_out,
    w_hi, w_lo, top_hi, top_lo, pheno_hi, pheno_lo, kept,
):
    step = pl.program_id(0)
    place = lax.axis_index("pcol") * own_out.shape[0]

    @pl.when(step == 0)
    def _():
        w_hi[...], w_lo[...] = split2(w_in[...])
        w = (w_hi[...], w_lo[...])
        white = dot3(w, split2(top_in[...]), INNER)
        top_hi[...], top_lo[...] = split2(white)
        row = jnp.broadcast_to(pheno_in[...], pheno_hi.shape)
        pheno = split2(dot3(split2(row), w, LAST))
        pheno_hi[...], pheno_lo[...] = pheno
        stat_out[...] = jnp.zeros_like(stat_out)
        stat_out[2:3, :] = dot3(pheno, (top_hi[...], top_lo[...]), INNER)[:1]
        stat_out[3:4, :] = jnp.sum(white * white, axis=0, keepdims=True)

    w = (w_hi[...], w_lo[...])
    panel = dot3(split2(rows_in[...]), w, LAST)
    parts = split2(panel)
    hi_out[...], lo_out[...] = parts

    @pl.when(place // tile == step)
    def _():
        kept[...] = panel
        start = pl.multiple_of(lax.rem(place, tile), TILE)
        own_out[...] = kept[pl.ds(start, own_out.shape[0]), :]

    @pl.when(step < col_tiles)
    def _():
        col_hi_out[...], col_lo_out[...] = split2(dot3(w, split2(cols_in[...]), LAST))

    white = geno_in[...] - dot3(parts, (top_hi[...], top_lo[...]), INNER)
    geno_out[...] = white
    pheno = rest_in[0] - dot3((pheno_hi[...], pheno_lo[...]), parts, LAST)
    stat_out[0:1, :] += dot3(split2(pheno), split2(white), INNER)[:1]
    stat_out[1:2, :] += jnp.sum(white * white, axis=0, keepdims=True)


def whiten(inverse, top, pheno, rows, cols, geno_rest, pheno_rest, rows_piece):
    width = inverse.shape[0]
    row_count, variants = geno_rest.shape
    col_count = cols.shape[0]
    tile = min(256, row_count)
    col_tile = min(256, col_count)
    steps, col_tiles = row_count // tile, col_count // col_tile
    f32, bf16 = jnp.float32, jnp.bfloat16
    rest = pheno_rest.reshape(steps, 1, tile)

    def fixed(shape):
        return pl.BlockSpec(shape, lambda i: (0,) * len(shape))

    def by_row(wide):
        return pl.BlockSpec((tile, wide), lambda i: (i, 0))

    last = col_tiles - 1
    col_out = pl.BlockSpec((width, col_tile), lambda i: (0, jnp.minimum(i, last)))
    return pl.pallas_call(
        functools.partial(whiten_kernel, tile, rows_piece, col_tiles),
        grid=(steps,),
        in_specs=[
            fixed((width, width)),
            fixed((width, variants)),
            fixed((1, width)),
            by_row(width),
            pl.BlockSpec((col_tile, width), lambda i: (jnp.minimum(i, last), 0)),
            by_row(variants),
            pl.BlockSpec((1, 1, tile), lambda i: (i, 0, 0)),
        ],
        out_specs=(
            by_row(width), by_row(width), col_out, col_out,
            fixed((rows_piece, width)), by_row(variants), fixed((8, variants)),
        ),
        out_shape=(
            jax.ShapeDtypeStruct((row_count, width), bf16),
            jax.ShapeDtypeStruct((row_count, width), bf16),
            jax.ShapeDtypeStruct((width, col_count), bf16),
            jax.ShapeDtypeStruct((width, col_count), bf16),
            jax.ShapeDtypeStruct((rows_piece, width), f32),
            jax.ShapeDtypeStruct((row_count, variants), f32),
            jax.ShapeDtypeStruct((8, variants), f32),
        ),
        scratch_shapes=[
            pltpu.VMEM((width, width), bf16),
            pltpu.VMEM((width, width), bf16),
            pltpu.VMEM((width, variants), bf16),
            pltpu.VMEM((width, variants), bf16),
            pltpu.VMEM((16, width), bf16),
            pltpu.VMEM((16, width), bf16),
            pltpu.VMEM((tile, width), f32),
        ],
        compiler_params=pltpu.CompilerParams(vmem_limit_bytes=40 * 1024 * 1024),
        cost_estimate=pl.CostEstimate(
            flops=6 * width * width * (row_count + col_count),
            bytes_accessed=16 * 1024 * 1024,
            transcendentals=0,
        ),
    )(inverse, top, pheno, rows, cols, geno_rest, rest)


def update_kernel(hi_in, lo_in, col_hi_in, col_lo_in, trailing_in, out):
    right = (col_hi_in[...], col_lo_in[...])
    out[...] = trailing_in[...] - dot3((hi_in[...], lo_in[...]), right, INNER)


def update(hi, lo, col_hi, col_lo, trailing):
    row_count, col_count = trailing.shape
    width = hi.shape[1]
    tile = min(256, row_count)
    left = pl.BlockSpec((tile, width), lambda i: (i, 0))
    right = pl.BlockSpec((width, col_count), lambda i: (0, 0))
    block = pl.BlockSpec((tile, col_count), lambda i: (i, 0))
    return pl.pallas_call(
        update_kernel,
        grid=(row_count // tile,),
        in_specs=[left, left, right, right, block],
        out_specs=block,
        out_shape=jax.ShapeDtypeStruct(trailing.shape, jnp.float32),
        compiler_params=pltpu.CompilerParams(vmem_limit_bytes=40 * 1024 * 1024),
        cost_estimate=pl.CostEstimate(
            flops=6 * width * row_count * col_count,
            bytes_accessed=20 * 1024 * 1024,
            transcendentals=0,
        ),
    )(hi, lo, col_hi, col_lo, trailing)


def local(diag_block, panel_cols, trailing, geno_top, geno_rest, pheno_top, pheno_rest):
    prow_size, pcol_size = lax.axis_size("prow"), lax.axis_size("pcol")
    height, width = diag_block.shape
    rows_piece = panel_cols.shape[0]
    row_count = rows_piece * pcol_size
    variants = geno_top.shape[1]
    inverse, whole, col_raw, top_all, pheno_all = gather_and_invert(
        diag_block, geno_top, pheno_top.reshape(1, height), panel_cols, prow_size, pcol_size
    )
    hi, lo, col_hi, col_lo, own_factor, white_geno, stats = whiten(
        inverse,
        top_all.reshape(width, variants),
        pheno_all.reshape(1, width),
        whole.reshape(row_count, width),
        col_raw.reshape(-1, width),
        geno_rest,
        pheno_rest,
        rows_piece,
    )

    def fetch(flip):
        return lax.ppermute(stats, "prow", [(i, i ^ flip) for i in range(prow_size)])

    sib, cross, diag = fetch(1), fetch(2), fetch(3)
    updated_block = update(hi, lo, col_hi, col_lo, trailing)
    total = (stats + sib) + (cross + diag)
    count = jnp.float32(width + row_count * prow_size)
    score_stat = (total[0] + stats[2]) / jnp.sqrt(count)
    info_stat = (total[1] + stats[3]) / count
    return (updated_block, own_factor, white_geno, score_stat, info_stat)


def solution(mesh):
    placed = (
        P("prow", None),
        P(("prow", "pcol"), None),
        P("prow", "pcol"),
        P("prow", "pcol"),
        P("prow", "pcol"),
        P("prow"),
        P("prow"),
    )
    return jax.shard_map(
        local,
        mesh=mesh,
        in_specs=placed,
        out_specs=(
            P("prow", "pcol"),
            P(("prow", "pcol"), None),
            P("prow", "pcol"),
            P("pcol"),
            P("pcol"),
        ),
        check_vma=False,
    )
```

```python
import functools

import jax
import jax.numpy as jnp
from jax import lax
from jax.experimental import pallas as pl
from jax.experimental.pallas import tpu as pltpu
from jax.sharding import PartitionSpec as P

MESH = pl.DeviceIdType.MESH
HIGHEST = lax.Precision.HIGHEST
TILE = 16
PARTS = 4
BLOCK = 128


def split3(value):
    hi = value.astype(jnp.bfloat16).astype(jnp.float32)
    rest = value - hi
    mid = rest.astype(jnp.bfloat16).astype(jnp.float32)
    return hi, mid, rest - mid


def tile_step(m_ref, step):
    start = pl.multiple_of(step * TILE, TILE)
    left = m_ref[pl.ds(start, TILE), :BLOCK]
    right = m_ref[pl.ds(start, TILE), BLOCK:]
    rolled = pltpu.roll(left, lax.rem(BLOCK - start, BLOCK), 1)
    cols = [jnp.broadcast_to(rolled[:, k : k + 1], (TILE, BLOCK)) for k in range(TILE)]
    rows = lax.broadcasted_iota(jnp.int32, (TILE, BLOCK), 0)
    lanes = lax.broadcasted_iota(jnp.int32, (TILE, BLOCK), 1)
    pivots = jnp.zeros_like(left)
    for j in range(TILE):
        pivot = jnp.broadcast_to(cols[j][j : j + 1, :], (TILE, BLOCK))
        inv = pl.reciprocal(pivot, approx=True)
        inv = inv * (2.0 - pivot * inv)
        below = jnp.where(rows > j, cols[j], 0.0)
        pivots = jnp.where(rows == j, pivot, pivots)

        def work(value):
            return value - below * (jnp.broadcast_to(value[j : j + 1, :], (TILE, BLOCK)) * inv)

        for k in range(j + 1, TILE):
            cols[k] = work(cols[k])
        left, right = work(left), work(right)
    scale = lax.rsqrt(pivots)
    scale = scale * (1.5 - (0.5 * pivots) * scale * scale)
    left, right = left * scale, right * scale
    m_ref[pl.ds(start, TILE), :BLOCK] = left
    m_ref[pl.ds(start, TILE), BLOCK:] = right
    both = jnp.concatenate([left, right], axis=1)
    mult = jnp.where(lanes >= start + TILE, left, 0.0)
    a0, a1, a2 = split3(mult)
    b0, b1, b2 = split3(both)
    lhs = jnp.concatenate([a0, a0, a1, a0, a1, a2], axis=0).astype(jnp.bfloat16)
    rhs = jnp.concatenate([b0, b1, b0, b2, b1, b0], axis=0).astype(jnp.bfloat16)
    m_ref[...] -= lax.dot_general(
        lhs, rhs, (((0,), (0,)), ((), ())), preferred_element_type=jnp.float32
    )


def dot_t(a, b):
    return lax.dot_general(
        a, b, (((0,), (0,)), ((), ())), precision=HIGHEST, preferred_element_type=jnp.float32
    )


def dot_n(a, b):
    return jnp.dot(a, b, precision=HIGHEST, preferred_element_type=jnp.float32)


def invert(a_ref, w_ref, m_ref, events):
    width = a_ref.shape[0]
    blocks = width // BLOCK
    tiles = BLOCK // TILE
    w_ref[...] = jnp.zeros_like(w_ref)
    eye = (
        lax.broadcasted_iota(jnp.int32, (BLOCK, BLOCK), 0)
        == lax.broadcasted_iota(jnp.int32, (BLOCK, BLOCK), 1)
    ).astype(jnp.float32)
    slot = 0
    for k in range(blocks):
        lo, hi = k * BLOCK, (k + 1) * BLOCK
        m_ref[:, :BLOCK] = a_ref[lo:hi, lo:hi]
        m_ref[:, BLOCK:] = eye
        for part in range(PARTS):

            def body(step, carry):
                tile_step(m_ref, step)
                return carry

            lax.fori_loop(part * tiles // PARTS, (part + 1) * tiles // PARTS, body, 0)
            if part < PARTS - 1:
                if slot < len(events):
                    events[slot]()
                slot += 1
        own = m_ref[:, BLOCK:]
        if k > 0:
            w_ref[lo:hi, :lo] = dot_n(own, w_ref[lo:hi, :lo])
        w_ref[lo:hi, lo:hi] = own
        if k < blocks - 1:
            upper = dot_n(own, a_ref[lo:hi, hi:])
            a_ref[hi:, hi:] -= dot_t(upper, upper)
            w_ref[hi:, :hi] -= dot_t(upper, w_ref[lo:hi, :hi])
        if slot < len(events):
            events[slot]()
        slot += 1
    while slot < len(events):
        events[slot]()
        slot += 1


def gather_kernel(
    ly, lz, group,
    diag_in, top_in, pheno_in, panel_in,
    w_out, row_out, col_out, top_out, pheno_out,
    a_ref, m_ref,
    small_send, small_recv, row_send, row_recv, col_send, col_recv, local_sem,
):
    r, c = lax.axis_index("prow"), lax.axis_index("pcol")
    z, y = c // ly, lax.rem(c, ly)
    sib = r + 1 - 2 * lax.rem(r, 2)
    cross = r + 2 - 4 * (r // 2)
    diag_x = sib + 2 - 4 * (sib // 2)
    other = z * ly + (1 - y)
    col_parts = col_out.shape[0]
    root = c // group
    first = lax.rem(c, group) * col_parts
    is_root = root == r
    root_cross = root + 2 - 4 * (root // 2)

    barrier = pltpu.get_barrier_semaphore()

    def greet(row, col):
        pl.semaphore_signal(barrier, inc=1, device_id={"prow": row, "pcol": col}, device_id_type=MESH)

    greet(sib, c)
    greet(cross, c)
    greet(r, other)

    @pl.when(z > 0)
    def _():
        greet(r, c - ly)

    @pl.when(z < lz - 1)
    def _():
        greet(r, c + ly)

    pl.semaphore_wait(barrier, 3 + jnp.minimum(z, 1) + jnp.minimum(lz - 1 - z, 1))

    def remote(src, dst, send, recv, row, col):
        return pltpu.make_async_remote_copy(
            src_ref=src, dst_ref=dst, send_sem=send, recv_sem=recv,
            device_id={"prow": row, "pcol": col}, device_id_type=MESH,
        )

    height = diag_in.shape[0]

    def diag_at(q):
        return a_ref.at[pl.ds(pl.multiple_of(q * height, height), height), :]

    places = (diag_at, lambda q: top_out.at[q], lambda q: pheno_out.at[q])

    def small(kind, lane):
        source = (diag_in, top_in, pheno_in)[kind]
        place = places[kind]
        part = cross if lane == 2 else r
        src = place(part) if lane == 2 else source
        return remote(
            src, place(part), small_send.at[kind, lane], small_recv.at[kind, part],
            cross if lane == 1 else sib, c,
        )

    def small_wait(kind, part):
        place = places[kind]
        remote(place(part), place(part), small_send.at[kind, 0], small_recv.at[kind, part], sib, c).wait_recv()

    def row_copy(way, b, own):
        target = (c + ly, c - ly, other)[way]
        return remote(
            panel_in if own else row_out.at[b], row_out.at[b],
            row_send.at[way, b], row_recv.at[b], r, target,
        )

    def row_wait(b):
        remote(row_out.at[b], row_out.at[b], row_send.at[0, b], row_recv.at[b], r, other).wait_recv()

    def col_copies(b, own):
        i = b - first
        src = panel_in if own else row_out.at[b]
        return (
            remote(src, col_out.at[i], col_send.at[0, i], col_recv.at[i], cross, c),
            remote(src, col_out.at[i], col_send.at[1, i], col_recv.at[i], sib, c),
            pltpu.make_async_copy(src, col_out.at[i], local_sem.at[1 + i]),
        )

    def in_col(b):
        return is_root & (b >= first) & (b < first + col_parts)

    def col_start(b, own):
        @pl.when(in_col(b))
        def _():
            for copy in col_copies(b, own):
                copy.start()

    def col_finish(b, own):
        @pl.when(in_col(b))
        def _():
            one, two, three = col_copies(b, own)
            one.wait_send()
            two.wait_send()
            three.wait()

    def up(fn):
        pl.when(z < lz - 1)(fn)

    def down(fn):
        pl.when(z > 0)(fn)

    small(0, 1).start()
    small(0, 0).start()
    row_copy(2, c, True).start()
    up(lambda: row_copy(0, c, True).start())
    down(lambda: row_copy(1, c, True).start())
    for kind in (1, 2):
        small(kind, 1).start()
        small(kind, 0).start()
    own_copy = pltpu.make_async_copy(panel_in, row_out.at[c], local_sem.at[0])
    own_copy.start()
    top_copy = pltpu.make_async_copy(top_in, top_out.at[r], local_sem.at[1 + col_parts])
    top_copy.start()
    pheno_copy = pltpu.make_async_copy(pheno_in, pheno_out.at[r], local_sem.at[2 + col_parts])
    pheno_copy.start()
    diag_copy = pltpu.make_async_copy(diag_in, diag_at(r), local_sem.at[3 + col_parts])
    diag_copy.start()
    col_start(c, True)
    small_wait(0, cross)
    small(0, 2).start()
    small_wait(0, sib)
    small_wait(0, diag_x)
    diag_copy.wait()
    small(0, 2).wait_send()

    def hop(d):
        low, high = c - d * ly, c + d * ly

        @pl.when(z >= d)
        def _():
            row_wait(low)
            up(lambda: row_copy(0, low, False).start())
            row_copy(2, low, False).start()
            col_start(low, False)

        @pl.when(z + d < lz)
        def _():
            row_wait(high)
            down(lambda: row_copy(1, high, False).start())
            row_copy(2, high, False).start()
            col_start(high, False)

    def across(d):
        def one(b):
            row_wait(b)
            col_start(b, False)

        if d == 0:
            one(other)
        else:
            pl.when(z >= d)(lambda: one(other - d * ly))
            pl.when(z + d < lz)(lambda: one(other + d * ly))

    def top_event():
        for kind in (1, 2):
            small_wait(kind, cross)
            small(kind, 2).start()

    def nothing():
        pass

    def hop_at(d):
        return functools.partial(hop, d) if d < lz else nothing

    def across_at(d):
        return functools.partial(across, d) if d < lz else nothing

    events = [hop_at(1), across_at(0), top_event, nothing, hop_at(2), nothing, nothing, nothing]
    events += [hop_at(3), across_at(1), nothing, nothing, across_at(2), nothing, nothing, nothing]
    for d in range(4, lz):
        events += [hop_at(d), across_at(d - 1)]
    events.append(across_at(lz - 1))
    invert(a_ref, w_out, m_ref, events)

    def handed(i):
        return remote(col_out.at[i], col_out.at[i], col_send.at[1, i], col_recv.at[i], sib, c)

    @pl.when(r == root_cross)
    def _():
        for i in range(col_parts):
            handed(i).wait_recv()
            handed(i).start()
        for i in range(col_parts):
            handed(i).wait_send()

    @pl.when(jnp.logical_not(is_root) & (r != root_cross))
    def _():
        for i in range(col_parts):
            handed(i).wait_recv()

    small(0, 1).wait_send()
    small(0, 0).wait_send()
    for kind in (1, 2):
        for lane in range(3):
            small(kind, lane).wait_send()
        small_wait(kind, sib)
        small_wait(kind, diag_x)
    own_copy.wait()
    top_copy.wait()
    pheno_copy.wait()
    row_copy(2, c, True).wait_send()
    up(lambda: row_copy(0, c, True).wait_send())
    down(lambda: row_copy(1, c, True).wait_send())
    col_finish(c, True)
    col_finish(other, False)
    for d in range(1, lz):

        @pl.when(z >= d)
        def _():
            low = c - d * ly
            up(lambda: row_copy(0, low, False).wait_send())
            row_copy(2, low, False).wait_send()
            col_finish(low, False)
            col_finish(other - d * ly, False)

        @pl.when(z + d < lz)
        def _():
            high = c + d * ly
            down(lambda: row_copy(1, high, False).wait_send())
            row_copy(2, high, False).wait_send()
            col_finish(high, False)
            col_finish(other + d * ly, False)


def gather_and_invert(diag_block, geno_top, pheno_row, panel_cols, prow_size, pcol_size):
    ly = 2
    lz = pcol_size // ly
    height, width = diag_block.shape
    rows_piece = panel_cols.shape[0]
    col_parts = prow_size
    any_spec = pl.BlockSpec(memory_space=pl.ANY)
    vmem = pl.BlockSpec(memory_space=pltpu.VMEM)
    dma = pltpu.SemaphoreType.DMA
    f32 = jnp.float32
    return pl.pallas_call(
        functools.partial(gather_kernel, ly, lz, pcol_size // prow_size),
        out_shape=(
            jax.ShapeDtypeStruct((width, width), f32),
            jax.ShapeDtypeStruct((pcol_size, rows_piece, width), f32),
            jax.ShapeDtypeStruct((col_parts, rows_piece, width), f32),
            jax.ShapeDtypeStruct((prow_size,) + geno_top.shape, f32),
            jax.ShapeDtypeStruct((prow_size,) + pheno_row.shape, f32),
        ),
        in_specs=[pl.BlockSpec(memory_space=pltpu.HBM)] * 4,
        out_specs=(vmem, any_spec, any_spec, any_spec, any_spec),
        scratch_shapes=[
            pltpu.VMEM((width, width), f32),
            pltpu.VMEM((BLOCK, 2 * BLOCK), f32),
            dma((3, 3)),
            dma((3, prow_size)),
            dma((3, pcol_size)),
            dma((pcol_size,)),
            dma((2, col_parts)),
            dma((col_parts,)),
            dma((4 + col_parts,)),
        ],
        compiler_params=pltpu.CompilerParams(
            collective_id=0, has_side_effects=True, vmem_limit_bytes=24 * 1024 * 1024
        ),
    )(diag_block, geno_top, pheno_row, panel_cols)


LAST = ((1,), (1,))
INNER = ((1,), (0,))


def split2(value):
    hi = value.astype(jnp.bfloat16)
    return hi, (value - hi.astype(jnp.float32)).astype(jnp.bfloat16)


def dot3(a, b, dims):
    left = jnp.concatenate([a[0], a[0], a[1]], axis=dims[0][0])
    right = jnp.concatenate([b[0], b[1], b[0]], axis=dims[1][0])
    return lax.dot_general(left, right, (dims, ((), ())), preferred_element_type=jnp.float32)


def whiten_kernel(
    tile, pieces, col_tiles,
    w_in, top_in, pheno_in, rows_in, cols_in, geno_in, rest_in,
    hi_out, lo_out, col_hi_out, col_lo_out, own_out, geno_out, stat_out,
    w_hi, w_lo, top_hi, top_lo, pheno_hi, pheno_lo, kept,
):
    step = pl.program_id(0)
    place = lax.axis_index("pcol") * own_out.shape[0]

    @pl.when(step == 0)
    def _():
        w_hi[...], w_lo[...] = split2(w_in[...])
        w = (w_hi[...], w_lo[...])
        white = dot3(w, split2(top_in[...]), INNER)
        top_hi[...], top_lo[...] = split2(white)
        row = jnp.broadcast_to(pheno_in[...], pheno_hi.shape)
        pheno = split2(dot3(split2(row), w, LAST))
        pheno_hi[...], pheno_lo[...] = pheno
        stat_out[...] = jnp.zeros_like(stat_out)
        stat_out[2:3, :] = dot3(pheno, (top_hi[...], top_lo[...]), INNER)[:1]
        stat_out[3:4, :] = jnp.sum(white * white, axis=0, keepdims=True)

    w = (w_hi[...], w_lo[...])
    panel = dot3(split2(rows_in[...]), w, LAST)
    parts = split2(panel)
    hi_out[...], lo_out[...] = parts

    @pl.when(place // tile == step)
    def _():
        kept[...] = panel
        start = pl.multiple_of(lax.rem(place, tile), TILE)
        own_out[...] = kept[pl.ds(start, own_out.shape[0]), :]

    @pl.when(step < col_tiles)
    def _():
        col_hi_out[...], col_lo_out[...] = split2(dot3(w, split2(cols_in[...]), LAST))

    white = geno_in[...] - dot3(parts, (top_hi[...], top_lo[...]), INNER)
    geno_out[...] = white
    pheno = rest_in[0] - dot3((pheno_hi[...], pheno_lo[...]), parts, LAST)
    stat_out[0:1, :] += dot3(split2(pheno), split2(white), INNER)[:1]
    stat_out[1:2, :] += jnp.sum(white * white, axis=0, keepdims=True)


def whiten(inverse, top, pheno, rows, cols, geno_rest, pheno_rest, rows_piece):
    width = inverse.shape[0]
    row_count, variants = geno_rest.shape
    col_count = cols.shape[0]
    tile = min(256, row_count)
    col_tile = min(256, col_count)
    steps, col_tiles = row_count // tile, col_count // col_tile
    f32, bf16 = jnp.float32, jnp.bfloat16
    rest = pheno_rest.reshape(steps, 1, tile)

    def fixed(shape):
        return pl.BlockSpec(shape, lambda i: (0,) * len(shape))

    def by_row(wide):
        return pl.BlockSpec((tile, wide), lambda i: (i, 0))

    last = col_tiles - 1
    col_out = pl.BlockSpec((width, col_tile), lambda i: (0, jnp.minimum(i, last)))
    return pl.pallas_call(
        functools.partial(whiten_kernel, tile, rows_piece, col_tiles),
        grid=(steps,),
        in_specs=[
            fixed((width, width)),
            fixed((width, variants)),
            fixed((1, width)),
            by_row(width),
            pl.BlockSpec((col_tile, width), lambda i: (jnp.minimum(i, last), 0)),
            by_row(variants),
            pl.BlockSpec((1, 1, tile), lambda i: (i, 0, 0)),
        ],
        out_specs=(
            by_row(width), by_row(width), col_out, col_out,
            fixed((rows_piece, width)), by_row(variants), fixed((8, variants)),
        ),
        out_shape=(
            jax.ShapeDtypeStruct((row_count, width), bf16),
            jax.ShapeDtypeStruct((row_count, width), bf16),
            jax.ShapeDtypeStruct((width, col_count), bf16),
            jax.ShapeDtypeStruct((width, col_count), bf16),
            jax.ShapeDtypeStruct((rows_piece, width), f32),
            jax.ShapeDtypeStruct((row_count, variants), f32),
            jax.ShapeDtypeStruct((8, variants), f32),
        ),
        scratch_shapes=[
            pltpu.VMEM((width, width), bf16),
            pltpu.VMEM((width, width), bf16),
            pltpu.VMEM((width, variants), bf16),
            pltpu.VMEM((width, variants), bf16),
            pltpu.VMEM((16, width), bf16),
            pltpu.VMEM((16, width), bf16),
            pltpu.VMEM((tile, width), f32),
        ],
        compiler_params=pltpu.CompilerParams(vmem_limit_bytes=20 * 1024 * 1024),
        cost_estimate=pl.CostEstimate(
            flops=6 * width * width * (row_count + col_count),
            bytes_accessed=16 * 1024 * 1024,
            transcendentals=0,
        ),
    )(inverse, top, pheno, rows, cols, geno_rest, rest)


def update_kernel(hi_in, lo_in, col_hi_in, col_lo_in, trailing_in, out):
    right = (col_hi_in[...], col_lo_in[...])
    out[...] = trailing_in[...] - dot3((hi_in[...], lo_in[...]), right, INNER)


def update(hi, lo, col_hi, col_lo, trailing):
    row_count, col_count = trailing.shape
    width = hi.shape[1]
    tile = min(256, row_count)
    left = pl.BlockSpec((tile, width), lambda i: (i, 0))
    right = pl.BlockSpec((width, col_count), lambda i: (0, 0))
    block = pl.BlockSpec((tile, col_count), lambda i: (i, 0))
    return pl.pallas_call(
        update_kernel,
        grid=(row_count // tile,),
        in_specs=[left, left, right, right, block],
        out_specs=block,
        out_shape=jax.ShapeDtypeStruct(trailing.shape, jnp.float32),
        compiler_params=pltpu.CompilerParams(vmem_limit_bytes=20 * 1024 * 1024),
        cost_estimate=pl.CostEstimate(
            flops=6 * width * row_count * col_count,
            bytes_accessed=20 * 1024 * 1024,
            transcendentals=0,
        ),
    )(hi, lo, col_hi, col_lo, trailing)


def local(diag_block, panel_cols, trailing, geno_top, geno_rest, pheno_top, pheno_rest):
    prow_size, pcol_size = lax.axis_size("prow"), lax.axis_size("pcol")
    height, width = diag_block.shape
    rows_piece = panel_cols.shape[0]
    row_count = rows_piece * pcol_size
    variants = geno_top.shape[1]
    inverse, whole, col_raw, top_all, pheno_all = gather_and_invert(
        diag_block, geno_top, pheno_top.reshape(1, height), panel_cols, prow_size, pcol_size
    )
    hi, lo, col_hi, col_lo, own_factor, white_geno, stats = whiten(
        inverse,
        top_all.reshape(width, variants),
        pheno_all.reshape(1, width),
        whole.reshape(row_count, width),
        col_raw.reshape(-1, width),
        geno_rest,
        pheno_rest,
        rows_piece,
    )

    def fetch(flip):
        return lax.ppermute(stats, "prow", [(i, i ^ flip) for i in range(prow_size)])

    sib, cross, diag = fetch(1), fetch(2), fetch(3)
    updated_block = update(hi, lo, col_hi, col_lo, trailing)
    total = (stats + sib) + (cross + diag)
    count = jnp.float32(width + row_count * prow_size)
    score_stat = (total[0] + stats[2]) / jnp.sqrt(count)
    info_stat = (total[1] + stats[3]) / count
    return (updated_block, own_factor, white_geno, score_stat, info_stat)


def solution(mesh):
    placed = (
        P("prow", None),
        P(("prow", "pcol"), None),
        P("prow", "pcol"),
        P("prow", "pcol"),
        P("prow", "pcol"),
        P("prow"),
        P("prow"),
    )
    return jax.shard_map(
        local,
        mesh=mesh,
        in_specs=placed,
        out_specs=(
            P("prow", "pcol"),
            P(("prow", "pcol"), None),
            P("prow", "pcol"),
            P("pcol"),
            P("pcol"),
        ),
        check_vma=False,
    )
```

```python
import functools

import jax
import jax.numpy as jnp
from jax import lax
from jax.experimental import pallas as pl
from jax.experimental.pallas import tpu as pltpu
from jax.sharding import PartitionSpec as P

MESH = pl.DeviceIdType.MESH
HIGHEST = lax.Precision.HIGHEST
TILE = 16
PARTS = 4
BLOCK = 128


def split3(value):
    hi = value.astype(jnp.bfloat16).astype(jnp.float32)
    rest = value - hi
    mid = rest.astype(jnp.bfloat16).astype(jnp.float32)
    return hi, mid, rest - mid


def tile_step(m_ref, step):
    start = pl.multiple_of(step * TILE, TILE)
    left = m_ref[pl.ds(start, TILE), :BLOCK]
    right = m_ref[pl.ds(start, TILE), BLOCK:]
    rolled = pltpu.roll(left, lax.rem(BLOCK - start, BLOCK), 1)
    cols = [jnp.broadcast_to(rolled[:, k : k + 1], (TILE, BLOCK)) for k in range(TILE)]
    rows = lax.broadcasted_iota(jnp.int32, (TILE, BLOCK), 0)
    lanes = lax.broadcasted_iota(jnp.int32, (TILE, BLOCK), 1)
    pivots = jnp.zeros_like(left)
    for j in range(TILE):
        pivot = jnp.broadcast_to(cols[j][j : j + 1, :], (TILE, BLOCK))
        inv = pl.reciprocal(pivot, approx=True)
        inv = inv * (2.0 - pivot * inv)
        below = jnp.where(rows > j, cols[j], 0.0)
        pivots = jnp.where(rows == j, pivot, pivots)

        def work(value):
            return value - below * (jnp.broadcast_to(value[j : j + 1, :], (TILE, BLOCK)) * inv)

        for k in range(j + 1, TILE):
            cols[k] = work(cols[k])
        left, right = work(left), work(right)
    scale = lax.rsqrt(pivots)
    scale = scale * (1.5 - (0.5 * pivots) * scale * scale)
    left, right = left * scale, right * scale
    m_ref[pl.ds(start, TILE), :BLOCK] = left
    m_ref[pl.ds(start, TILE), BLOCK:] = right
    both = jnp.concatenate([left, right], axis=1)
    mult = jnp.where(lanes >= start + TILE, left, 0.0)
    a0, a1, a2 = split3(mult)
    b0, b1, b2 = split3(both)
    lhs = jnp.concatenate([a0, a0, a1, a0, a1, a2], axis=0).astype(jnp.bfloat16)
    rhs = jnp.concatenate([b0, b1, b0, b2, b1, b0], axis=0).astype(jnp.bfloat16)
    m_ref[...] -= lax.dot_general(
        lhs, rhs, (((0,), (0,)), ((), ())), preferred_element_type=jnp.float32
    )


def dot_t(a, b):
    return lax.dot_general(
        a, b, (((0,), (0,)), ((), ())), precision=HIGHEST, preferred_element_type=jnp.float32
    )


def dot_n(a, b):
    return jnp.dot(a, b, precision=HIGHEST, preferred_element_type=jnp.float32)


def invert(a_ref, w_ref, m_ref, events):
    width = a_ref.shape[0]
    blocks = width // BLOCK
    tiles = BLOCK // TILE
    w_ref[...] = jnp.zeros_like(w_ref)
    eye = (
        lax.broadcasted_iota(jnp.int32, (BLOCK, BLOCK), 0)
        == lax.broadcasted_iota(jnp.int32, (BLOCK, BLOCK), 1)
    ).astype(jnp.float32)
    slot = 0
    for k in range(blocks):
        lo, hi = k * BLOCK, (k + 1) * BLOCK
        m_ref[:, :BLOCK] = a_ref[lo:hi, lo:hi]
        m_ref[:, BLOCK:] = eye
        for part in range(PARTS):

            def body(step, carry):
                tile_step(m_ref, step)
                return carry

            lax.fori_loop(part * tiles // PARTS, (part + 1) * tiles // PARTS, body, 0)
            if part < PARTS - 1:
                if slot < len(events):
                    events[slot]()
                slot += 1
        own = m_ref[:, BLOCK:]
        if k > 0:
            w_ref[lo:hi, :lo] = dot_n(own, w_ref[lo:hi, :lo])
        w_ref[lo:hi, lo:hi] = own
        if k < blocks - 1:
            upper = dot_n(own, a_ref[lo:hi, hi:])
            a_ref[hi:, hi:] -= dot_t(upper, upper)
            w_ref[hi:, :hi] -= dot_t(upper, w_ref[lo:hi, :hi])
        if slot < len(events):
            events[slot]()
        slot += 1
    while slot < len(events):
        events[slot]()
        slot += 1


def gather_kernel(
    ly, lz, group,
    diag_in, top_in, pheno_in, panel_in,
    w_out, row_out, col_out, top_out, pheno_out,
    a_ref, m_ref,
    small_send, small_recv, row_send, row_recv, col_send, col_recv, local_sem,
):
    r, c = lax.axis_index("prow"), lax.axis_index("pcol")
    z, y = c // ly, lax.rem(c, ly)
    sib = r + 1 - 2 * lax.rem(r, 2)
    cross = r + 2 - 4 * (r // 2)
    diag_x = sib + 2 - 4 * (sib // 2)
    other = z * ly + (1 - y)
    col_parts = col_out.shape[0]
    root = c // group
    first = lax.rem(c, group) * col_parts
    is_root = root == r
    root_cross = root + 2 - 4 * (root // 2)

    barrier = pltpu.get_barrier_semaphore()

    def greet(row, col):
        pl.semaphore_signal(barrier, inc=1, device_id={"prow": row, "pcol": col}, device_id_type=MESH)

    greet(sib, c)
    greet(cross, c)
    greet(r, other)

    @pl.when(z > 0)
    def _():
        greet(r, c - ly)

    @pl.when(z < lz - 1)
    def _():
        greet(r, c + ly)

    pl.semaphore_wait(barrier, 3 + jnp.minimum(z, 1) + jnp.minimum(lz - 1 - z, 1))

    def remote(src, dst, send, recv, row, col):
        return pltpu.make_async_remote_copy(
            src_ref=src, dst_ref=dst, send_sem=send, recv_sem=recv,
            device_id={"prow": row, "pcol": col}, device_id_type=MESH,
        )

    height = diag_in.shape[0]

    def diag_at(q):
        return a_ref.at[pl.ds(pl.multiple_of(q * height, height), height), :]

    places = (diag_at, lambda q: top_out.at[q], lambda q: pheno_out.at[q])

    def small(kind, lane):
        source = (diag_in, top_in, pheno_in)[kind]
        place = places[kind]
        part = cross if lane == 2 else r
        src = place(part) if lane == 2 else source
        return remote(
            src, place(part), small_send.at[kind, lane], small_recv.at[kind, part],
            cross if lane == 1 else sib, c,
        )

    def small_wait(kind, part):
        place = places[kind]
        remote(place(part), place(part), small_send.at[kind, 0], small_recv.at[kind, part], sib, c).wait_recv()

    def row_copy(way, b, own):
        target = (c + ly, c - ly, other)[way]
        return remote(
            panel_in if own else row_out.at[b], row_out.at[b],
            row_send.at[way, b], row_recv.at[b], r, target,
        )

    def row_wait(b):
        remote(row_out.at[b], row_out.at[b], row_send.at[0, b], row_recv.at[b], r, other).wait_recv()

    def col_copies(b, own):
        i = b - first
        src = panel_in if own else row_out.at[b]
        return (
            remote(src, col_out.at[i], col_send.at[0, i], col_recv.at[i], cross, c),
            remote(src, col_out.at[i], col_send.at[1, i], col_recv.at[i], sib, c),
            pltpu.make_async_copy(src, col_out.at[i], local_sem.at[1 + i]),
        )

    def in_col(b):
        return is_root & (b >= first) & (b < first + col_parts)

    def col_start(b, own):
        @pl.when(in_col(b))
        def _():
            for copy in col_copies(b, own):
                copy.start()

    def col_finish(b, own):
        @pl.when(in_col(b))
        def _():
            one, two, three = col_copies(b, own)
            one.wait_send()
            two.wait_send()
            three.wait()

    def up(fn):
        pl.when(z < lz - 1)(fn)

    def down(fn):
        pl.when(z > 0)(fn)

    small(0, 1).start()
    small(0, 0).start()
    row_copy(2, c, True).start()
    up(lambda: row_copy(0, c, True).start())
    down(lambda: row_copy(1, c, True).start())
    for kind in (1, 2):
        small(kind, 1).start()
        small(kind, 0).start()
    own_copy = pltpu.make_async_copy(panel_in, row_out.at[c], local_sem.at[0])
    own_copy.start()
    top_copy = pltpu.make_async_copy(top_in, top_out.at[r], local_sem.at[1 + col_parts])
    top_copy.start()
    pheno_copy = pltpu.make_async_copy(pheno_in, pheno_out.at[r], local_sem.at[2 + col_parts])
    pheno_copy.start()
    diag_copy = pltpu.make_async_copy(diag_in, diag_at(r), local_sem.at[3 + col_parts])
    diag_copy.start()
    col_start(c, True)
    small_wait(0, cross)
    small(0, 2).start()
    small_wait(0, sib)
    small_wait(0, diag_x)
    diag_copy.wait()
    small(0, 2).wait_send()

    def hop(d):
        low, high = c - d * ly, c + d * ly

        @pl.when(z >= d)
        def _():
            row_wait(low)
            up(lambda: row_copy(0, low, False).start())
            row_copy(2, low, False).start()
            col_start(low, False)

        @pl.when(z + d < lz)
        def _():
            row_wait(high)
            down(lambda: row_copy(1, high, False).start())
            row_copy(2, high, False).start()
            col_start(high, False)

    def across(d):
        def one(b):
            row_wait(b)
            col_start(b, False)

        if d == 0:
            one(other)
        else:
            pl.when(z >= d)(lambda: one(other - d * ly))
            pl.when(z + d < lz)(lambda: one(other + d * ly))

    def top_event():
        for kind in (1, 2):
            small_wait(kind, cross)
            small(kind, 2).start()

    def nothing():
        pass

    def hop_at(d):
        return functools.partial(hop, d) if d < lz else nothing

    def across_at(d):
        return functools.partial(across, d) if d < lz else nothing

    events = [hop_at(1), across_at(0), top_event, nothing, hop_at(2), nothing, nothing, nothing]
    events += [nothing, across_at(1), hop_at(3), nothing, nothing, across_at(2), nothing, nothing]
    for d in range(4, lz):
        events += [hop_at(d), across_at(d - 1)]
    events.append(across_at(lz - 1))
    invert(a_ref, w_out, m_ref, events)

    def handed(i):
        return remote(col_out.at[i], col_out.at[i], col_send.at[1, i], col_recv.at[i], sib, c)

    @pl.when(r == root_cross)
    def _():
        for i in range(col_parts):
            handed(i).wait_recv()
            handed(i).start()
        for i in range(col_parts):
            handed(i).wait_send()

    @pl.when(jnp.logical_not(is_root) & (r != root_cross))
    def _():
        for i in range(col_parts):
            handed(i).wait_recv()

    small(0, 1).wait_send()
    small(0, 0).wait_send()
    for kind in (1, 2):
        for lane in range(3):
            small(kind, lane).wait_send()
        small_wait(kind, sib)
        small_wait(kind, diag_x)
    own_copy.wait()
    top_copy.wait()
    pheno_copy.wait()
    row_copy(2, c, True).wait_send()
    up(lambda: row_copy(0, c, True).wait_send())
    down(lambda: row_copy(1, c, True).wait_send())
    col_finish(c, True)
    col_finish(other, False)
    for d in range(1, lz):

        @pl.when(z >= d)
        def _():
            low = c - d * ly
            up(lambda: row_copy(0, low, False).wait_send())
            row_copy(2, low, False).wait_send()
            col_finish(low, False)
            col_finish(other - d * ly, False)

        @pl.when(z + d < lz)
        def _():
            high = c + d * ly
            down(lambda: row_copy(1, high, False).wait_send())
            row_copy(2, high, False).wait_send()
            col_finish(high, False)
            col_finish(other + d * ly, False)


def gather_and_invert(diag_block, geno_top, pheno_row, panel_cols, prow_size, pcol_size):
    ly = 2
    lz = pcol_size // ly
    height, width = diag_block.shape
    rows_piece = panel_cols.shape[0]
    col_parts = prow_size
    any_spec = pl.BlockSpec(memory_space=pl.ANY)
    vmem = pl.BlockSpec(memory_space=pltpu.VMEM)
    dma = pltpu.SemaphoreType.DMA
    f32 = jnp.float32
    return pl.pallas_call(
        functools.partial(gather_kernel, ly, lz, pcol_size // prow_size),
        out_shape=(
            jax.ShapeDtypeStruct((width, width), f32),
            jax.ShapeDtypeStruct((pcol_size, rows_piece, width), f32),
            jax.ShapeDtypeStruct((col_parts, rows_piece, width), f32),
            jax.ShapeDtypeStruct((prow_size,) + geno_top.shape, f32),
            jax.ShapeDtypeStruct((prow_size,) + pheno_row.shape, f32),
        ),
        in_specs=[pl.BlockSpec(memory_space=pltpu.HBM)] * 4,
        out_specs=(vmem, any_spec, any_spec, any_spec, any_spec),
        scratch_shapes=[
            pltpu.VMEM((width, width), f32),
            pltpu.VMEM((BLOCK, 2 * BLOCK), f32),
            dma((3, 3)),
            dma((3, prow_size)),
            dma((3, pcol_size)),
            dma((pcol_size,)),
            dma((2, col_parts)),
            dma((col_parts,)),
            dma((4 + col_parts,)),
        ],
        compiler_params=pltpu.CompilerParams(
            collective_id=0, has_side_effects=True, vmem_limit_bytes=24 * 1024 * 1024
        ),
    )(diag_block, geno_top, pheno_row, panel_cols)


LAST = ((1,), (1,))
INNER = ((1,), (0,))


def split2(value):
    hi = value.astype(jnp.bfloat16)
    return hi, (value - hi.astype(jnp.float32)).astype(jnp.bfloat16)


def dot3(a, b, dims):
    left = jnp.concatenate([a[0], a[0], a[1]], axis=dims[0][0])
    right = jnp.concatenate([b[0], b[1], b[0]], axis=dims[1][0])
    return lax.dot_general(left, right, (dims, ((), ())), preferred_element_type=jnp.float32)


def column(row):
    return jnp.transpose(jnp.broadcast_to(row, (BLOCK, row.shape[1])))


def weighted(weights, values):
    wide = jnp.concatenate([weights] * (values.shape[1] // BLOCK), axis=1)
    return jnp.sum(wide * values, axis=0, keepdims=True)


def whiten_kernel(
    tile, pieces, col_tiles,
    w_in, top_in, pheno_in, rows_in, cols_in, geno_in, rest_in,
    hi_out, lo_out, col_hi_out, col_lo_out, own_out, geno_out, stat_out,
    w_hi, w_lo, turned_hi, turned_lo, top_hi, top_lo, kept,
):
    step = pl.program_id(0)
    place = lax.axis_index("pcol") * own_out.shape[0]
    variants = geno_in.shape[1]

    @pl.when(step == 0)
    def _():
        w_hi[...], w_lo[...] = split2(w_in[...])
        w = (w_hi[...], w_lo[...])
        turned_hi[...], turned_lo[...] = split2(jnp.transpose(w_in[...]))
        joined = jnp.concatenate([top_in[...], column(pheno_in[...])], axis=1)
        both = dot3(w, split2(joined), INNER)
        top_hi[...], top_lo[...] = split2(both)
        white = both[:, :variants]
        stat_out[...] = jnp.zeros_like(stat_out)
        stat_out[2:3, :] = weighted(both[:, variants:], white)
        stat_out[3:4, :] = jnp.sum(white * white, axis=0, keepdims=True)

    w = (w_hi[...], w_lo[...])
    panel = dot3(split2(rows_in[...]), (turned_hi[...], turned_lo[...]), INNER)
    parts = split2(panel)
    hi_out[...], lo_out[...] = parts

    @pl.when(place // tile == step)
    def _():
        kept[...] = panel
        start = pl.multiple_of(lax.rem(place, tile), TILE)
        own_out[...] = kept[pl.ds(start, own_out.shape[0]), :]

    @pl.when(step < col_tiles)
    def _():
        col_hi_out[...], col_lo_out[...] = split2(dot3(w, split2(cols_in[...]), LAST))

    shift = dot3(parts, (top_hi[...], top_lo[...]), INNER)
    white = geno_in[...] - shift[:, :variants]
    geno_out[...] = white
    stat_out[0:1, :] += weighted(column(rest_in[0]) - shift[:, variants:], white)
    stat_out[1:2, :] += jnp.sum(white * white, axis=0, keepdims=True)


def whiten(inverse, top, pheno, rows, cols, geno_rest, pheno_rest, rows_piece):
    width = inverse.shape[0]
    row_count, variants = geno_rest.shape
    col_count = cols.shape[0]
    tile = min(256, row_count)
    col_tile = min(256, col_count)
    steps, col_tiles = row_count // tile, col_count // col_tile
    f32, bf16 = jnp.float32, jnp.bfloat16
    rest = pheno_rest.reshape(steps, 1, tile)

    def fixed(shape):
        return pl.BlockSpec(shape, lambda i: (0,) * len(shape))

    def by_row(wide):
        return pl.BlockSpec((tile, wide), lambda i: (i, 0))

    last = col_tiles - 1
    col_out = pl.BlockSpec((width, col_tile), lambda i: (0, jnp.minimum(i, last)))
    return pl.pallas_call(
        functools.partial(whiten_kernel, tile, rows_piece, col_tiles),
        grid=(steps,),
        in_specs=[
            fixed((width, width)),
            fixed((width, variants)),
            fixed((1, width)),
            by_row(width),
            pl.BlockSpec((col_tile, width), lambda i: (jnp.minimum(i, last), 0)),
            by_row(variants),
            pl.BlockSpec((1, 1, tile), lambda i: (i, 0, 0)),
        ],
        out_specs=(
            by_row(width), by_row(width), col_out, col_out,
            fixed((rows_piece, width)), by_row(variants), fixed((8, variants)),
        ),
        out_shape=(
            jax.ShapeDtypeStruct((row_count, width), bf16),
            jax.ShapeDtypeStruct((row_count, width), bf16),
            jax.ShapeDtypeStruct((width, col_count), bf16),
            jax.ShapeDtypeStruct((width, col_count), bf16),
            jax.ShapeDtypeStruct((rows_piece, width), f32),
            jax.ShapeDtypeStruct((row_count, variants), f32),
            jax.ShapeDtypeStruct((8, variants), f32),
        ),
        scratch_shapes=[
            pltpu.VMEM((width, width), bf16),
            pltpu.VMEM((width, width), bf16),
            pltpu.VMEM((width, width), bf16),
            pltpu.VMEM((width, width), bf16),
            pltpu.VMEM((width, variants + BLOCK), bf16),
            pltpu.VMEM((width, variants + BLOCK), bf16),
            pltpu.VMEM((tile, width), f32),
        ],
        compiler_params=pltpu.CompilerParams(vmem_limit_bytes=20 * 1024 * 1024),
        cost_estimate=pl.CostEstimate(
            flops=6 * width * width * (row_count + col_count),
            bytes_accessed=16 * 1024 * 1024,
            transcendentals=0,
        ),
    )(inverse, top, pheno, rows, cols, geno_rest, rest)


def update_kernel(hi_in, lo_in, col_hi_in, col_lo_in, trailing_in, out):
    right = (col_hi_in[...], col_lo_in[...])
    out[...] = trailing_in[...] - dot3((hi_in[...], lo_in[...]), right, INNER)


def update(hi, lo, col_hi, col_lo, trailing):
    row_count, col_count = trailing.shape
    width = hi.shape[1]
    tile = min(256, row_count)
    left = pl.BlockSpec((tile, width), lambda i: (i, 0))
    right = pl.BlockSpec((width, col_count), lambda i: (0, 0))
    block = pl.BlockSpec((tile, col_count), lambda i: (i, 0))
    return pl.pallas_call(
        update_kernel,
        grid=(row_count // tile,),
        in_specs=[left, left, right, right, block],
        out_specs=block,
        out_shape=jax.ShapeDtypeStruct(trailing.shape, jnp.float32),
        compiler_params=pltpu.CompilerParams(vmem_limit_bytes=20 * 1024 * 1024),
        cost_estimate=pl.CostEstimate(
            flops=6 * width * row_count * col_count,
            bytes_accessed=20 * 1024 * 1024,
            transcendentals=0,
        ),
    )(hi, lo, col_hi, col_lo, trailing)


def local(diag_block, panel_cols, trailing, geno_top, geno_rest, pheno_top, pheno_rest):
    prow_size, pcol_size = lax.axis_size("prow"), lax.axis_size("pcol")
    height, width = diag_block.shape
    rows_piece = panel_cols.shape[0]
    row_count = rows_piece * pcol_size
    variants = geno_top.shape[1]
    inverse, whole, col_raw, top_all, pheno_all = gather_and_invert(
        diag_block, geno_top, pheno_top.reshape(1, height), panel_cols, prow_size, pcol_size
    )
    hi, lo, col_hi, col_lo, own_factor, white_geno, stats = whiten(
        inverse,
        top_all.reshape(width, variants),
        pheno_all.reshape(1, width),
        whole.reshape(row_count, width),
        col_raw.reshape(-1, width),
        geno_rest,
        pheno_rest,
        rows_piece,
    )

    def fetch(flip):
        return lax.ppermute(stats, "prow", [(i, i ^ flip) for i in range(prow_size)])

    sib, cross, diag = fetch(1), fetch(2), fetch(3)
    updated_block = update(hi, lo, col_hi, col_lo, trailing)
    total = (stats + sib) + (cross + diag)
    count = jnp.float32(width + row_count * prow_size)
    score_stat = (total[0] + stats[2]) / jnp.sqrt(count)
    info_stat = (total[1] + stats[3]) / count
    return (updated_block, own_factor, white_geno, score_stat, info_stat)


def solution(mesh):
    placed = (
        P("prow", None),
        P(("prow", "pcol"), None),
        P("prow", "pcol"),
        P("prow", "pcol"),
        P("prow", "pcol"),
        P("prow"),
        P("prow"),
    )
    return jax.shard_map(
        local,
        mesh=mesh,
        in_specs=placed,
        out_specs=(
            P("prow", "pcol"),
            P(("prow", "pcol"), None),
            P("prow", "pcol"),
            P("pcol"),
            P("pcol"),
        ),
        check_vma=False,
    )
```
